256 devices in a mesh: section: 8 (over y, z_lo), dp: 32 (over z_hi, x, core).
Axes of the slice: x: 4, y: 4, z: 8 (z_hi: 4, z_lo: 2; z = z_hi * 2 + z_lo), core: 2. Of those that a mesh axis runs over, the one named last changes fastest.
Arguments:
- frames: bfloat16 [4, 32, 128, 2560], P(None, 'dp'), may hold values from -170 to 170
- gains: float32 [8, 2560], P('section'), may hold values from 0.1 to 1.9
- w_shared: bfloat16 [8, 2560, 2560], P('section', 'dp'), may hold values from -0.125 to 0.125
- temper: float32 [8, 20], P('section'), may hold values from 0.25 to 32
Outputs:
- saved: bfloat16 [8, 4, 32, 128, 2560], P('section', None, 'dp')
The draws below stay inside these ranges and needn't reach their ends.
All inputs are finite; a program needn't handle non-finite values.
Results may differ from the reference program's by a relative error of at most 0.008.
Values may be sent and summed in bfloat16 or wider, within the bound.
A program may use at most 64 MiB of HBM per device.

```python
import math
import jax
import jax.numpy as jnp
from jax import lax

HEADS = 20
D = 2560
FR = 128
MICRO = 4
SECTIONS = 8
BATCH = 32


def draw_frames(key, part):
    key = jax.random.fold_in(key, 11)
    base_key = jax.random.fold_in(key, 0)
    shape = (MICRO, BATCH, FR, D)
    base = jax.random.normal(base_key, shape, jnp.float32)
    return base.astype(jnp.bfloat16)


def draw_temper(key, part):
    key = jax.random.fold_in(key, 23)
    value = jax.random.uniform(key, (SECTIONS, HEADS), jnp.float32, math.log(0.25), math.log(2.0))
    return jnp.exp(value)


def block_scale(key, dims, cuts, smallest, high):
    level = 1.0
    for axis_at, blocks in cuts:
        draws = jax.random.uniform(jax.random.fold_in(jax.random.fold_in(key, 6), axis_at), (blocks,), jnp.float32, smallest / len(cuts), high / len(cuts))
        level = level * jnp.repeat(jnp.exp(draws), dims[axis_at] // blocks).reshape((-1,) + (1,) * (len(dims) - 1 - axis_at))
    return level


def scatter_about(rng, shape, scale, limit, pieces=(), dtype=jnp.bfloat16):
    drawn = jax.random.normal(rng, shape, jnp.float32) * scale
    if len(pieces) > 0:
        drawn = block_scale(rng, shape, pieces, -0.22, 0.18) * drawn
    return jnp.clip(drawn, min=-limit, max=limit).astype(dtype)


def setup_inputs(seed: int = 0) -> dict:
    splits = jax.random.split(jax.random.key(seed), 5)
    frames = draw_frames(jax.random.fold_in(splits[4], 71), 0)
    gains = jnp.clip(1.0 + 0.18 * jax.random.normal(splits[1], (SECTIONS, D), jnp.float32), 0.1, 1.9)
    w_shared = scatter_about(splits[2], (SECTIONS, D, D), D ** -0.5, 0.125, ((0, 8), (1, 32)))
    temper = draw_temper(jax.random.fold_in(splits[4], 71), 0)
    return {"frames": frames, "gains": gains, "w_shared": w_shared, "temper": temper}


def attend_layer(x, gain, weight, temper_row):
    count = x.shape[0]
    frame_count = x.shape[1]
    width = x.shape[2]
    heads = temper_row.shape[0]
    head_size = width // heads
    x_wide = x.astype(jnp.float32)
    scale = lax.rsqrt(lax.optimization_barrier(jnp.mean(x_wide * x_wide, axis=-1, keepdims=True)) + 1e-05)
    normed = (x_wide * scale * gain).astype(jnp.bfloat16)
    proj = jnp.dot(normed.reshape(count * frame_count, width), weight, preferred_element_type=jnp.float32)
    proj = proj.astype(jnp.bfloat16).reshape(count, frame_count, heads, head_size).astype(jnp.float32)
    values = normed.reshape(count, frame_count, heads, head_size).astype(jnp.float32)
    scores = jnp.einsum('bqhd,bkhd->bhqk', proj, proj)
    scores = scores * (temper_row / jnp.sqrt(jnp.float32(head_size)))[None, :, None, None]
    rows = lax.broadcasted_iota(jnp.int32, (frame_count, frame_count), 0)
    cols = lax.broadcasted_iota(jnp.int32, (frame_count, frame_count), 1)
    keep = (cols < rows) | (rows == 0) & (cols == 0)
    scores = jnp.where(keep[None, None], scores, jnp.float32(-1e+30))
    top = lax.optimization_barrier(jnp.max(scores, axis=-1, keepdims=True))
    expo = jnp.exp(scores - top)
    weights = (expo / lax.optimization_barrier(jnp.sum(expo, axis=-1, keepdims=True))).astype(jnp.bfloat16)
    mixed = jnp.einsum('bhqk,bkhd->bqhd', weights.astype(jnp.float32), values)
    return (x_wide + mixed.reshape(count, frame_count, width)).astype(jnp.bfloat16)

def reference(frames, gains, w_shared, temper):
    per_micro = []
    for micro in range(MICRO):
        state = frames[micro]
        layer_outs = []
        for layer in range(SECTIONS):
            state = attend_layer(state, gains[layer], w_shared[layer], temper[layer])
            layer_outs.append(state)
        per_micro.append(jnp.stack(layer_outs[::-1], axis=0))
    return jnp.stack(per_micro, axis=1)
```

```python
import functools

import jax
import jax.numpy as jnp
from jax import lax
from jax.experimental import pallas as pl
from jax.experimental.pallas import tpu as pltpu
from jax.sharding import PartitionSpec as P

MESH = pl.DeviceIdType.MESH
F32 = jnp.float32
BF16 = jnp.bfloat16

D = 2560
FR = 128
LAYERS = 8
PLANES = 4
QD = D // PLANES
HEAD = 128
QH = QD // HEAD
NX = 4
NZH = 4
ROWS = 80


def kernel(
    frames, w_in, gt_in, out,
    w, xs, nrm, gt,
    w1s, w1r, zs, zr, x_s, x_r, cs, cr, ys, yr, gs, gr, fl, ol, os_, or_,
):
    sec = lax.axis_index("section")
    dp = lax.axis_index("dp")
    y = sec // 2
    zl = sec % 2
    zh = dp // 8
    x = (dp // 2) % NX
    c = dp % 2
    z = zh * 2 + zl

    def at_y(q):
        return (q * 2 + zl, dp)

    def at_x(xx):
        return (sec, zh * 8 + xx * 2 + c)

    def at_z(zz):
        return (y * 2 + zz % 2, (zz // 2) * 8 + x * 2 + c)

    sibling = (sec, zh * 8 + x * 2 + 1 - c)
    pair = (y * 2 + 1 - zl, dp)

    peers = [at_y((y + d) % PLANES) for d in range(1, PLANES)]
    peers += [at_x((x + d) % NX) for d in range(1, NX)]
    peers += [at_z((z + d) % 8) for d in range(1, 8)]
    peers += [sibling]
    peers += [(((y + d) % PLANES) * 2 + 1 - zl, dp) for d in range(1, PLANES)]
    barrier = pltpu.get_barrier_semaphore()
    for p in peers:
        pl.semaphore_signal(barrier, inc=1, device_id=p, device_id_type=MESH)
    pl.semaphore_wait(barrier, len(peers))

    def remote(src, dst, s, r, to):
        return pltpu.make_async_remote_copy(
            src_ref=src, dst_ref=dst, send_sem=s, recv_sem=r, device_id=to, device_id_type=MESH
        )

    def w1_copy(d):
        q = (y + d) % PLANES
        return remote(
            w_in.at[0, :, pl.ds(pl.multiple_of(q * QD, QD), QD)],
            w.at[sec, zh, x, c],
            w1s.at[d - 1], w1r.at[d - 1], at_y(q),
        )

    def w1_own():
        return pltpu.make_async_copy(
            w_in.at[0, :, pl.ds(pl.multiple_of(y * QD, QD), QD)], w.at[sec, zh, x, c], w1s.at[3]
        )

    def z_copy(p, d):
        l = 2 * p + zl
        return remote(
            w.at[l, zh, x, c], w.at[l, zh, x, c], zs.at[p, d - 1], zr.at[l, zh], at_z((z + d) % 8)
        )

    def z_arrival(l, h):
        return remote(w.at[l, h, x, c], w.at[l, h, x, c], zs.at[0, 0], zr.at[l, h], pair)

    def x_copy(l, d):
        return remote(
            w.at[l, :, x, c], w.at[l, :, x, c], x_s.at[l, d - 1], x_r.at[l, d - 1], at_x((x + d) % NX)
        )

    def c_copy(l):
        return remote(w.at[l, :, :, c], w.at[l, :, :, c], cs.at[l], cr.at[l], sibling)

    def y_copy(l, u, d):
        return remote(
            xs.at[l, u, y], xs.at[l, u, y], ys.at[l - 1, u, d - 1], yr.at[l - 1, u, d - 1], at_y((y + d) % PLANES)
        )

    def g_copy(j):
        s = (sec + j) % LAYERS
        return remote(gt_in, gt.at[sec], gs.at[j - 1], gr.at[j - 1], (s, dp))

    def frame_copy(u, q):
        return pltpu.make_async_copy(
            frames.at[2 * zl + u, 0, :, pl.ds(q * QD, QD)], xs.at[0, u, q], fl.at[u, q]
        )

    for d in range(1, PLANES):
        w1_copy(d).start()
    w1_own().start()
    for u in range(2):
        for q in range(PLANES):
            frame_copy(u, q).start()
    for j in range(1, LAYERS):
        g_copy(j).start()
    gt[sec] = gt_in[...]

    def w1_to_z(p):
        for d in range(1, PLANES):
            @pl.when((y - d) % PLANES == p)
            def _():
                w1_copy(d).wait_recv()

        @pl.when(y == p)
        def _():
            w1_own().wait()

        for d in range(1, 8):
            z_copy(p, d).start()

    def z_to_x(l):
        for h in range(NZH):
            @pl.when((l % 2 != zl) | (zh != h))
            def _():
                z_arrival(l, h).wait_recv()
        for d in range(1, NX):
            x_copy(l, d).start()

    def x_to_c(l):
        for d in range(1, NX):
            x_copy(l, d).wait_recv()
        c_copy(l).start()

    w1_to_z(0)
    w1_to_z(1)
    z_to_x(0)
    z_to_x(1)
    w1_to_z(2)
    x_to_c(0)
    w1_to_z(3)
    for u in range(2):
        for q in range(PLANES):
            frame_copy(u, q).wait()
    for j in range(1, LAYERS):
        g_copy(j).wait_recv()

    own_saved = LAYERS - 1 - sec
    pair_saved = LAYERS - 1 - pair[0]

    def out_at(ref, m, q):
        return ref.at[0, m, 0, :, pl.ds(q * QD, QD)]

    def own_save(l, u, q):
        return pltpu.make_async_copy(xs.at[l, u, q], out_at(out, 2 * zl + u, q), ol.at[u, q])

    def pair_save(l, u, q):
        return remote(xs.at[l, u, q], out_at(out, 2 * zl + u, q), os_.at[u, q], or_.at[u, q], pair)

    def saves(l, u):
        @pl.when(l == own_saved + 1)
        def _():
            for q in range(PLANES):
                own_save(l, u, q).start()

        @pl.when(l == pair_saved + 1)
        def _():
            for q in range(PLANES):
                pair_save(l, u, q).start()

    rows = lax.broadcasted_iota(jnp.int32, (FR, FR), 0)
    cols = lax.broadcasted_iota(jnp.int32, (FR, FR), 1)
    keep = (cols < rows) | ((rows == 0) & (cols == 0))

    def compute(l, u):
        parts = [xs[l, u, q].astype(F32) for q in range(PLANES)]
        square = sum(jnp.sum(p * p, axis=-1, keepdims=True) for p in parts)
        scale = lax.rsqrt(square * (1.0 / D) + 1e-05)
        for q in range(PLANES):
            nrm[q] = (parts[q] * scale * gt[l, 0:1, q * QD:(q + 1) * QD]).astype(BF16)
        lhs = jnp.concatenate([nrm[q] for q in range(PLANES)], axis=1)
        proj = jnp.dot(lhs, w[l].reshape(D, QD), preferred_element_type=F32).astype(BF16)
        values = nrm[y]
        temper = gt[l, 1:2, pl.ds(pl.multiple_of(y * QD, QD), QD)]
        heads = [proj[:, k * HEAD:(k + 1) * HEAD] for k in range(QH)]
        scores = [
            lax.dot_general(h, h, (((1,), (1,)), ((), ())), preferred_element_type=F32) for h in heads
        ]
        scores = [
            jnp.where(keep, s * temper[:, k * HEAD:(k + 1) * HEAD], -1e30) for k, s in enumerate(scores)
        ]
        tops = [jnp.max(s, axis=-1, keepdims=True) for s in scores]
        expo = [jnp.exp(s - t) for s, t in zip(scores, tops)]
        sums = [jnp.sum(e, axis=-1, keepdims=True) for e in expo]
        weights = [(e / s).astype(BF16) for e, s in zip(expo, sums)]
        mixed = [
            jnp.dot(wt, values[:, k * HEAD:(k + 1) * HEAD], preferred_element_type=F32)
            for k, wt in enumerate(weights)
        ]
        xs[l + 1, u, y] = (xs[l, u, y].astype(F32) + jnp.concatenate(mixed, axis=1)).astype(BF16)

    def layer(l, carry):
        c_copy(l).wait_recv()
        for u in range(2):
            @pl.when(l > 0)
            def _():
                for d in range(1, PLANES):
                    y_copy(l, u, d).wait_recv()
                saves(l, u)

            compute(l, u)
            for d in range(1, PLANES):
                y_copy(l + 1, u, d).start()

        @pl.when(l + 2 < LAYERS)
        def _():
            z_to_x(l + 2)

        @pl.when(l + 1 < LAYERS)
        def _():
            x_to_c(l + 1)

        return carry

    lax.fori_loop(0, LAYERS, layer, 0)

    for u in range(2):
        for d in range(1, PLANES):
            y_copy(LAYERS, u, d).wait_recv()
        saves(LAYERS, u)

    for d in range(1, PLANES):
        w1_copy(d).wait_send()
    for j in range(1, LAYERS):
        g_copy(j).wait_send()
    for p in range(4):
        for d in range(1, 8):
            z_copy(p, d).wait_send()

    def drain(l, carry):
        for d in range(1, NX):
            x_copy(l, d).wait_send()
        c_copy(l).wait_send()
        for u in range(2):
            for d in range(1, PLANES):
                y_copy(l + 1, u, d).wait_send()
        return carry

    lax.fori_loop(0, LAYERS, drain, 0)
    for u in range(2):
        for q in range(PLANES):
            own_save(0, u, q).wait()
            pair_save(0, u, q).wait_send()
            pair_save(0, u, q).wait_recv()


def local(frames, gains, w_shared, temper):
    scale = jnp.repeat(temper * (1.0 / jnp.sqrt(jnp.float32(HEAD))), HEAD, axis=1)
    gt_in = jnp.concatenate([gains, scale], axis=0)
    dma = pltpu.SemaphoreType.DMA
    any_space = pl.BlockSpec(memory_space=pl.ANY)
    return pl.pallas_call(
        kernel,
        out_shape=jax.ShapeDtypeStruct((1,) + frames.shape, BF16),
        in_specs=[any_space, any_space, pl.BlockSpec(memory_space=pltpu.VMEM)],
        out_specs=any_space,
        scratch_shapes=[
            pltpu.VMEM((LAYERS, NZH, NX, 2, ROWS, QD), BF16),
            pltpu.VMEM((LAYERS + 1, 2, PLANES, FR, QD), BF16),
            pltpu.VMEM((PLANES, FR, QD), BF16),
            pltpu.VMEM((LAYERS, 2, D), F32),
            dma((4,)), dma((3,)),
            dma((4, 7)), dma((LAYERS, NZH)),
            dma((LAYERS, 3)), dma((LAYERS, 3)),
            dma((LAYERS,)), dma((LAYERS,)),
            dma((LAYERS, 2, 3)), dma((LAYERS, 2, 3)),
            dma((LAYERS - 1,)), dma((LAYERS - 1,)),
            dma((2, PLANES)), dma((2, PLANES)),
            dma((2, PLANES)), dma((2, PLANES)),
        ],
        compiler_params=pltpu.CompilerParams(
            collective_id=0, has_side_effects=True, vmem_limit_bytes=58 << 20
        ),
    )(frames, w_shared, gt_in)


def solution(mesh):
    in_specs = (
        P(None, "dp", None, None),
        P("section", None),
        P("section", "dp", None),
        P("section", None),
    )
    out_specs = P("section", None, "dp", None, None)
    return jax.shard_map(local, mesh=mesh, in_specs=in_specs, out_specs=out_specs, check_vma=False)
```

```python
import functools

import jax
import jax.numpy as jnp
from jax import lax
from jax.experimental import pallas as pl
from jax.experimental.pallas import tpu as pltpu
from jax.sharding import PartitionSpec as P

MESH = pl.DeviceIdType.MESH
F32 = jnp.float32
BF16 = jnp.bfloat16

D = 2560
FR = 128
HF = FR // 2
LAYERS = 8
PLANES = 4
QD = D // PLANES
HEAD = 128
QH = QD // HEAD
NX = 4
NZH = 4
ROWS = 80


def kernel(
    frames, w_in, gains, temper_in, out,
    w, shard, xs, nrm, gt,
    w1s, w1r, sl, zs, zr, x1s, x1r, x2s, x2r, ps, pr, cs, cr, y1s, y1r, y2s, y2r, gs, gr, fl, ol, os_, or_, ls, lr, es, er, hs, hr, rr,
):
    sec = lax.axis_index("section")
    dp = lax.axis_index("dp")
    y = sec // 2
    zl = sec % 2
    zh = dp // 8
    x = (dp // 2) % NX
    c = dp % 2
    z = zh * 2 + zl

    def at_y(q):
        return (q * 2 + zl, dp)

    def at_x(xx):
        return (sec, zh * 8 + xx * 2 + c)

    def at_z(zz):
        return (y * 2 + zz % 2, (zz // 2) * 8 + x * 2 + c)

    sibling = (sec, zh * 8 + x * 2 + 1 - c)
    pair = (y * 2 + 1 - zl, dp)

    peers = [at_y((y + d) % PLANES) for d in range(1, PLANES)]
    peers += [at_x((x + 1) % NX), at_x((x + 3) % NX)]
    peers += [at_z((z + d) % 8) for d in range(1, 8)]
    peers += [sibling]
    peers += [(((y + d) % PLANES) * 2 + 1 - zl, dp) for d in range(1, PLANES)]
    barrier = pltpu.get_barrier_semaphore()
    for p in peers:
        pl.semaphore_signal(barrier, inc=1, device_id=p, device_id_type=MESH)
    pl.semaphore_wait(barrier, len(peers))

    def remote(src, dst, s, r, to):
        return pltpu.make_async_remote_copy(
            src_ref=src, dst_ref=dst, send_sem=s, recv_sem=r, device_id=to, device_id_type=MESH
        )

    def w1_copy(d):
        q = (y + d) % PLANES
        return remote(
            w_in.at[0, :, pl.ds(pl.multiple_of(q * QD, QD), QD)],
            shard.at[y],
            w1s.at[d - 1], w1r.at[d - 1], at_y(q),
        )

    def w1_own():
        return pltpu.make_async_copy(
            w_in.at[0, :, pl.ds(pl.multiple_of(y * QD, QD), QD)], shard.at[y], w1s.at[3]
        )

    def shard_copy(p):
        return pltpu.make_async_copy(shard.at[p], w.at[2 * p + zl, zh, x, c], sl.at[p])

    def z_copy(p, d):
        l = 2 * p + zl
        return remote(
            shard.at[p], w.at[l, zh, x, c], zs.at[p, d - 1], zr.at[l, zh], at_z((z + d) % 8)
        )

    def z_arrival(l, h):
        return remote(w.at[l, h, x, c], w.at[l, h, x, c], zs.at[0, 0], zr.at[l, h], pair)

    def x1_copy(l, i):
        return remote(
            w.at[l, :, x, c], w.at[l, :, x, c], x1s.at[l, i], x1r.at[l, i], at_x((x + 1 + 2 * i) % NX)
        )

    def x2_copy(l, i):
        half = w.at[l, 2 * i:2 * i + 2, (x + 3 - 2 * i) % NX, c]
        return remote(half, half, x2s.at[l, i], x2r.at[l, i], at_x((x + 1 + 2 * i) % NX))

    def p_copy(l, i, d):
        part = w.at[l, 2 * i:2 * i + 2, (x + d) % NX, c]
        return remote(
            part, part, ps.at[l // 2, i, d], pr.at[l // 2, i, d], at_z((z + 1 + 6 * i) % 8)
        )

    def c_copy(l, d):
        xx = (x + d) % NX
        return remote(w.at[l, :, xx, c], w.at[l, :, xx, c], cs.at[l, d], cr.at[l, d], sibling)

    def y1_copy(l, u, i):
        return remote(
            xs.at[l, u, y], xs.at[l, u, y], y1s.at[l - 1, u, i], y1r.at[l - 1, u, i],
            at_y((y + 1 + 2 * i) % PLANES),
        )

    def y2_copy(l, u, i):
        half = xs.at[l, u, (y + 3 - 2 * i) % PLANES, i * HF:(i + 1) * HF]
        return remote(
            half, half, y2s.at[l - 1, u, i], y2r.at[l - 1, u, i], at_y((y + 1 + 2 * i) % PLANES)
        )

    def g_copy(j):
        s = (sec + j) % LAYERS
        return remote(gt.at[sec], gt.at[sec], gs.at[j - 1], gr.at[j - 1], (s, dp))

    def frame_copy(u, q):
        return pltpu.make_async_copy(
            frames.at[2 * zl + u, 0, :, pl.ds(q * QD, QD)], xs.at[0, u, q], fl.at[u, q]
        )

    w1_own().start()

    @pl.when(y == 0)
    def _():
        for d in range(1, PLANES):
            w1_copy(d).start()

    for u in range(2):
        for q in range(PLANES):
            frame_copy(u, q).start()
    gt[sec, 0:1] = gains[...]
    tempers = temper_in[...] / (HEAD ** 0.5)
    for k in range(D // HEAD):
        gt[sec, 1:2, k * HEAD:(k + 1) * HEAD] = jnp.broadcast_to(tempers[:, k:k + 1], (1, HEAD))

    works = zl == c

    def z_sends(p, act):
        for d in range(1, 8):
            @pl.when((zl == 1) | (d % 2 == c))
            def _():
                act(z_copy(p, d))

    def w1_arrive(p):
        for d in range(1, PLANES):
            @pl.when((y - d) % PLANES == p)
            def _():
                w1_copy(d).wait_recv()

        @pl.when(y == p)
        def _():
            w1_own().wait()

    def z_issue(p):
        z_sends(p, lambda copy: copy.start())

        @pl.when((zl == 1) | (c == 0))
        def _():
            shard_copy(p).start()

    def w1_to_z(p):
        w1_arrive(p)
        z_issue(p)

    def z_to_x(l):
        @pl.when((l % 2 == 1) | works)
        def _():
            for h in range(NZH):
                @pl.when((l % 2 != zl) | (zh != h))
                def _():
                    z_arrival(l, h).wait_recv()

            @pl.when(l % 2 == zl)
            def _():
                shard_copy(l // 2).wait()

            for i in range(2):
                x1_copy(l, i).start()

    def x1_to_x2(l):
        @pl.when((l % 2 == 1) | works)
        def _():
            for i in range(2):
                x1_copy(l, i).wait_recv()
                x2_copy(l, i).start()

            @pl.when(l % 2 == 0)
            def _():
                for d in (0, 1, 3):
                    for i in range(2):
                        p_copy(l, i, d).start()

            for d in (0, 1, 3):
                c_copy(l, d).start()

    def x2_to_c(l):
        @pl.when((l % 2 == 1) | works)
        def _():
            for i in range(2):
                x2_copy(l, i).wait_recv()

            @pl.when(l % 2 == 0)
            def _():
                for i in range(2):
                    p_copy(l, i, 2).start()

            c_copy(l, 2).start()

        @pl.when((l % 2 == 0) & jnp.logical_not(works))
        def _():
            for d in (0, 1, 3, 2):
                for i in range(2):
                    p_copy(l, i, d).wait_recv()
                c_copy(l, d).start()

    w1_arrive(0)

    @pl.when(zl == 0)
    def _():
        z_issue(0)

    @pl.when(y != 0)
    def _():
        for d in range(1, PLANES):
            w1_copy(d).start()

    for j in range(1, LAYERS):
        g_copy(j).start()
    z_to_x(0)

    @pl.when(zl == 1)
    def _():
        z_issue(0)

    x1_to_x2(0)
    z_to_x(1)
    w1_to_z(1)
    for u in range(2):
        for q in range(PLANES):
            frame_copy(u, q).wait()
    for j in range(1, LAYERS):
        g_copy(j).wait_recv()

    own_saved = LAYERS - 1 - sec
    pair_saved = LAYERS - 1 - pair[0]

    def out_at(ref, m, q):
        return ref.at[0, m, 0, :, pl.ds(q * QD, QD)]

    def own_save(l, u, q):
        return pltpu.make_async_copy(xs.at[l, u, q], out_at(out, 2 * zl + u, q), ol.at[u, q])

    def pair_save(l, u, q):
        return remote(xs.at[l, u, q], out_at(out, 2 * zl + u, q), os_.at[u, q], or_.at[u, q], pair)

    top = xs.at[LAYERS]

    def last_copy(u):
        return remote(
            top.at[u, y],
            out.at[0, 2 * zl + u, 0, :, pl.ds(pl.multiple_of(y * QD, QD), QD)],
            ls.at[u], lr.at[u, zl, y], (0, dp),
        )

    def far_half(u, i):
        half = top.at[u, 2, i * HF:(i + 1) * HF]
        return remote(half, half, hs.at[u, i], hr.at[u], (2 + 4 * i, dp))

    def far_whole(u):
        return remote(top.at[u, 2], top.at[u, 2], ls.at[u], hr.at[u], (1, dp))

    def half_on(u):
        i = y // 2
        part = pl.ds(pl.multiple_of(i * HF, HF), HF)
        return remote(
            top.at[u, 2, part], out.at[0, u, 0, part, 2 * QD:3 * QD], hs.at[u, 0], rr.at[u, i], (0, dp)
        )

    def whole_on(u):
        return remote(top.at[u, 2], out_at(out, 2 + u, 2), hs.at[u, 0], lr.at[u, 1, 2], (0, dp))

    def half_arrival(u, i):
        return remote(
            top.at[u, 2, i * HF:(i + 1) * HF], out.at[0, u, 0, i * HF:(i + 1) * HF, 2 * QD:3 * QD],
            hs.at[u, 0], rr.at[u, i], (1, dp),
        )

    direct = (sec != 0) & (y != 2)
    halves_on = (sec == 2) | (sec == 6)

    def last_own(u):
        return pltpu.make_async_copy(xs.at[LAYERS, u, 0], out_at(out, u, 0), ls.at[u])

    def last_arrival(u, zz, q):
        return remote(
            xs.at[LAYERS, u, q], out_at(out, 2 * zz + u, q), ls.at[u], lr.at[u, zz, q], (1, dp)
        )

    def saves(l, first, last):
        def due(saved):
            return (saved >= first) & (saved <= last) & (l == 6)

        for u in range(2):
            @pl.when(due(own_saved) | (own_saved == 6) & (first == 5) & (l == 7))
            def _():
                for q in range(PLANES):
                    own_save(own_saved + 1, u, q).start()

            @pl.when(due(pair_saved))
            def _():
                for q in range(PLANES):
                    pair_save(pair_saved + 1, u, q).start()

    def late_copy(u):
        return remote(
            xs.at[LAYERS - 1, u, y],
            out.at[0, 2 * zl + u, 0, :, pl.ds(pl.multiple_of(y * QD, QD), QD)],
            es.at[u], er.at[u, y], (1, dp),
        )

    def late_arrival(u, q):
        return remote(
            xs.at[LAYERS - 1, u, q], out_at(out, u, q), es.at[u], er.at[u, q], (0, dp)
        )

    rows = lax.broadcasted_iota(jnp.int32, (FR, FR), 0)
    cols = lax.broadcasted_iota(jnp.int32, (FR, FR), 1)
    keep = (cols < rows) | ((rows == 0) & (cols == 0))

    def compute(l, u):
        parts = [xs[l, u, q].astype(F32) for q in range(PLANES)]
        square = sum(jnp.sum(p * p, axis=-1, keepdims=True) for p in parts)
        scale = lax.rsqrt(square * (1.0 / D) + 1e-05)
        for q in range(PLANES):
            nrm[q] = (parts[q] * scale * gt[l, 0:1, q * QD:(q + 1) * QD]).astype(BF16)
        lhs = jnp.concatenate([nrm[q] for q in range(PLANES)], axis=1)
        proj = jnp.dot(lhs, w[l].reshape(D, QD), preferred_element_type=F32).astype(BF16)
        values = nrm[y]
        temper = gt[l, 1:2, pl.ds(pl.multiple_of(y * QD, QD), QD)]
        heads = [proj[:, k * HEAD:(k + 1) * HEAD] for k in range(QH)]
        scores = [
            lax.dot_general(h, h, (((1,), (1,)), ((), ())), preferred_element_type=F32) for h in heads
        ]
        scores = [
            jnp.where(keep, s * temper[:, k * HEAD:(k + 1) * HEAD], -1e30) for k, s in enumerate(scores)
        ]
        tops = [jnp.max(s, axis=-1, keepdims=True) for s in scores]
        expo = [jnp.exp(s - t) for s, t in zip(scores, tops)]
        sums = [jnp.sum(e, axis=-1, keepdims=True) for e in expo]
        weights = [(e / s).astype(BF16) for e, s in zip(expo, sums)]
        mixed = [
            jnp.dot(wt, values[:, k * HEAD:(k + 1) * HEAD], preferred_element_type=F32)
            for k, wt in enumerate(weights)
        ]
        xs[l + 1, u, y] = (xs[l, u, y].astype(F32) + jnp.concatenate(mixed, axis=1)).astype(BF16)

    def state_in(l, u):
        @pl.when(l > 0)
        def _():
            for i in range(2):
                y1_copy(l, u, i).wait_recv()
                y2_copy(l, u, i).start()

    def step(l, u):
        @pl.when(l > 0)
        def _():
            for i in range(2):
                y2_copy(l, u, i).wait_recv()

        compute(l, u)

        @pl.when((l == LAYERS - 1) & (sec == 0))
        def _():
            last_own(u).start()

        @pl.when((l == LAYERS - 1) & direct)
        def _():
            last_copy(u).start()

        @pl.when((l == LAYERS - 1) & (sec == 4))
        def _():
            for i in range(2):
                far_half(u, i).start()

        @pl.when((l == LAYERS - 1) & (sec == 5))
        def _():
            far_whole(u).start()

        @pl.when(l + 1 < LAYERS)
        def _():
            for i in range(2):
                y1_copy(l + 1, u, i).start()

    def ahead(l):
        @pl.when(l + 2 < LAYERS)
        def _():
            z_to_x(l + 2)

        for p in (2, 3):
            @pl.when(l + 2 == 2 * p - 2)
            def _():
                w1_to_z(p)

    def layer(l, carry):
        x2_to_c(l)
        saves(l, 0, 4)
        state_in(l, 0)

        @pl.when((l > 0) & (l + 1 < LAYERS))
        def _():
            x1_to_x2(l + 1)

        state_in(l, 1)

        @pl.when(l > 0)
        def _():
            ahead(l)

        for d in range(NX):
            c_copy(l, d).wait_recv()
        step(l, 0)

        @pl.when(l == 0)
        def _():
            x1_to_x2(1)

        step(l, 1)

        @pl.when(l == 0)
        def _():
            ahead(0)

        saves(l, 5, 5)
        return carry

    lax.fori_loop(0, LAYERS, layer, 0)

    @pl.when(zl == 0)
    def _():
        for u in range(2):
            late_copy(u).start()

    @pl.when(halves_on)
    def _():
        for u in range(2):
            far_half(u, 0).wait_recv()
            half_on(u).start()

    @pl.when(sec == 1)
    def _():
        for u in range(2):
            far_whole(u).wait_recv()
            whole_on(u).start()

    for d in range(1, PLANES):
        w1_copy(d).wait_send()
    for j in range(1, LAYERS):
        g_copy(j).wait_send()
    for p in range(4):
        z_sends(p, lambda copy: copy.wait_send())

    def drain(l, carry):
        @pl.when((l % 2 == 1) | works)
        def _():
            for i in range(2):
                x1_copy(l, i).wait_send()
                x2_copy(l, i).wait_send()

        @pl.when((l % 2 == 0) & works)
        def _():
            for i in range(2):
                for d in range(NX):
                    p_copy(l, i, d).wait_send()

        for d in range(NX):
            c_copy(l, d).wait_send()

        @pl.when(l > 0)
        def _():
            for u in range(2):
                for i in range(2):
                    y1_copy(l, u, i).wait_send()
                    y2_copy(l, u, i).wait_send()

        return carry

    lax.fori_loop(0, LAYERS, drain, 0)

    @pl.when(sec != 0)
    def _():
        for u in range(2):
            for q in range(PLANES):
                own_save(0, u, q).wait()

    @pl.when(direct)
    def _():
        for u in range(2):
            last_copy(u).wait_send()

    @pl.when(sec == 4)
    def _():
        for u in range(2):
            for i in range(2):
                far_half(u, i).wait_send()

    @pl.when(sec == 5)
    def _():
        for u in range(2):
            far_whole(u).wait_send()

    @pl.when(halves_on)
    def _():
        for u in range(2):
            half_on(u).wait_send()

    @pl.when(sec == 1)
    def _():
        for u in range(2):
            whole_on(u).wait_send()

    @pl.when(sec > 1)
    def _():
        for u in range(2):
            for q in range(PLANES):
                pair_save(0, u, q).wait_send()
                pair_save(0, u, q).wait_recv()

    @pl.when(zl == 0)
    def _():
        for u in range(2):
            late_copy(u).wait_send()

    @pl.when(sec == 1)
    def _():
        for u in range(2):
            for q in range(PLANES):
                late_arrival(u, q).wait_recv()

    @pl.when(sec == 0)
    def _():
        for u in range(2):
            last_own(u).wait()
            for zz in range(2):
                for q in range(PLANES):
                    if (zz, q) not in ((0, 0), (0, 2)):
                        last_arrival(u, zz, q).wait_recv()
            for i in range(2):
                half_arrival(u, i).wait_recv()


def local(frames, gains, w_shared, temper):
    dma = pltpu.SemaphoreType.DMA
    any_space = pl.BlockSpec(memory_space=pl.ANY)
    return pl.pallas_call(
        kernel,
        out_shape=jax.ShapeDtypeStruct((1,) + frames.shape, BF16),
        in_specs=[any_space, any_space] + [pl.BlockSpec(memory_space=pltpu.VMEM)] * 2,
        out_specs=any_space,
        scratch_shapes=[
            pltpu.VMEM((LAYERS, NZH, NX, 2, ROWS, QD), BF16),
            pltpu.VMEM((PLANES, ROWS, QD), BF16),
            pltpu.VMEM((LAYERS + 1, 2, PLANES, FR, QD), BF16),
            pltpu.VMEM((PLANES, FR, QD), BF16),
            pltpu.VMEM((LAYERS, 2, D), F32),
            dma((4,)), dma((3,)), dma((4,)),
            dma((4, 7)), dma((LAYERS, NZH)),
            dma((LAYERS, 2)), dma((LAYERS, 2)),
            dma((LAYERS, 2)), dma((LAYERS, 2)),
            dma((LAYERS // 2, 2, NX)), dma((LAYERS // 2, 2, NX)),
            dma((LAYERS, 4)), dma((LAYERS, 4)),
            dma((LAYERS, 2, 2)), dma((LAYERS, 2, 2)),
            dma((LAYERS, 2, 2)), dma((LAYERS, 2, 2)),
            dma((LAYERS - 1,)), dma((LAYERS - 1,)),
            dma((2, PLANES)), dma((2, PLANES)),
            dma((2, PLANES)), dma((2, PLANES)),
            dma((2,)), dma((2, 2, PLANES)),
            dma((2,)), dma((2, PLANES)),
            dma((2, 2)), dma((2,)), dma((2, 2)),
        ],
        compiler_params=pltpu.CompilerParams(
            collective_id=0, has_side_effects=True, vmem_limit_bytes=58 << 20
        ),
    )(frames, w_shared, gains, temper)


def solution(mesh):
    in_specs = (
        P(None, "dp", None, None),
        P("section", None),
        P("section", "dp", None),
        P("section", None),
    )
    out_specs = P("section", None, "dp", None, None)
    return jax.shard_map(local, mesh=mesh, in_specs=in_specs, out_specs=out_specs, check_vma=False)
```

```python
import functools

import jax
import jax.numpy as jnp
from jax import lax
from jax.experimental import pallas as pl
from jax.experimental.pallas import tpu as pltpu
from jax.sharding import PartitionSpec as P

MESH = pl.DeviceIdType.MESH
F32 = jnp.float32
BF16 = jnp.bfloat16

D = 2560
FR = 128
HF = FR // 2
LAYERS = 8
PLANES = 4
QD = D // PLANES
HEAD = 128
QH = QD // HEAD
NX = 4
NZH = 4
ROWS = 80


def kernel(
    frames, w_in, gains, temper_in, out,
    w, shard, xs, nrm, gt,
    w1s, w1r, sl, zs, zr, x1s, x1r, x2s, x2r, ps, pr, cs, cr, y1s, y1r, y2s, y2r, gs, gr, fl, ol, os_, or_, ls, lr, es, er, hs, hr, rr, fr,
):
    sec = lax.axis_index("section")
    dp = lax.axis_index("dp")
    y = sec // 2
    zl = sec % 2
    zh = dp // 8
    x = (dp // 2) % NX
    c = dp % 2
    z = zh * 2 + zl

    def at_y(q):
        return (q * 2 + zl, dp)

    def at_x(xx):
        return (sec, zh * 8 + xx * 2 + c)

    def at_z(zz):
        return (y * 2 + zz % 2, (zz // 2) * 8 + x * 2 + c)

    sibling = (sec, zh * 8 + x * 2 + 1 - c)
    pair = (y * 2 + 1 - zl, dp)

    peers = [at_y((y + d) % PLANES) for d in range(1, PLANES)]
    peers += [at_x((x + 1) % NX), at_x((x + 3) % NX)]
    peers += [at_z((z + d) % 8) for d in range(1, 8)]
    peers += [sibling]
    peers += [(((y + d) % PLANES) * 2 + 1 - zl, dp) for d in range(1, PLANES)]
    barrier = pltpu.get_barrier_semaphore()
    for p in peers:
        pl.semaphore_signal(barrier, inc=1, device_id=p, device_id_type=MESH)
    pl.semaphore_wait(barrier, len(peers))

    def remote(src, dst, s, r, to):
        return pltpu.make_async_remote_copy(
            src_ref=src, dst_ref=dst, send_sem=s, recv_sem=r, device_id=to, device_id_type=MESH
        )

    def w1_copy(d):
        q = (y + d) % PLANES
        return remote(
            w_in.at[0, :, pl.ds(pl.multiple_of(q * QD, QD), QD)],
            shard.at[y],
            w1s.at[d - 1], w1r.at[d - 1], at_y(q),
        )

    def w1_own():
        return pltpu.make_async_copy(
            w_in.at[0, :, pl.ds(pl.multiple_of(y * QD, QD), QD)], shard.at[y], w1s.at[3]
        )

    def shard_copy(p):
        return pltpu.make_async_copy(shard.at[p], w.at[2 * p + zl, zh, x, c], sl.at[p])

    def z_copy(p, d):
        l = 2 * p + zl
        return remote(
            shard.at[p], w.at[l, zh, x, c], zs.at[p, d - 1], zr.at[l, zh], at_z((z + d) % 8)
        )

    def z_arrival(l, h):
        return remote(w.at[l, h, x, c], w.at[l, h, x, c], zs.at[0, 0], zr.at[l, h], pair)

    def x1_copy(l, i):
        return remote(
            w.at[l, :, x, c], w.at[l, :, x, c], x1s.at[l, i], x1r.at[l, i], at_x((x + 1 + 2 * i) % NX)
        )

    def x2_copy(l, i):
        half = w.at[l, 2 * i:2 * i + 2, (x + 3 - 2 * i) % NX, c]
        return remote(half, half, x2s.at[l, i], x2r.at[l, i], at_x((x + 1 + 2 * i) % NX))

    def p_copy(l, i, d):
        part = w.at[l, 2 * i:2 * i + 2, (x + d) % NX, c]
        return remote(
            part, part, ps.at[l // 2, i, d], pr.at[l // 2, i, d], at_z((z + 1 + 6 * i) % 8)
        )

    def c_copy(l, d):
        xx = (x + d) % NX
        return remote(w.at[l, :, xx, c], w.at[l, :, xx, c], cs.at[l, d], cr.at[l, d], sibling)

    def y1_copy(l, u, i):
        return remote(
            xs.at[l, u, y], xs.at[l, u, y], y1s.at[l - 1, u, i], y1r.at[l - 1, u, i],
            at_y((y + 1 + 2 * i) % PLANES),
        )

    def y2_copy(l, u, i):
        half = xs.at[l, u, (y + 3 - 2 * i) % PLANES, i * HF:(i + 1) * HF]
        return remote(
            half, half, y2s.at[l - 1, u, i], y2r.at[l - 1, u, i], at_y((y + 1 + 2 * i) % PLANES)
        )

    def g_copy(j):
        s = (sec + j) % LAYERS
        return remote(gt.at[sec], gt.at[sec], gs.at[j - 1], gr.at[j - 1], (s, dp))

    def frame_copy(u, q):
        return pltpu.make_async_copy(
            frames.at[2 * zl + u, 0, :, pl.ds(q * QD, QD)], xs.at[0, u, q], fl.at[u, q]
        )

    w1_own().start()

    @pl.when(y == 0)
    def _():
        for d in range(1, PLANES):
            w1_copy(d).start()

    for u in range(2):
        for q in range(PLANES):
            frame_copy(u, q).start()
    gt[sec, 0:1] = gains[...]
    tempers = temper_in[...] / (HEAD ** 0.5)
    for k in range(D // HEAD):
        gt[sec, 1:2, k * HEAD:(k + 1) * HEAD] = jnp.broadcast_to(tempers[:, k:k + 1], (1, HEAD))

    works = zl == c

    def z_sends(p, act):
        for d in range(1, 8):
            @pl.when((zl == 1) | (d % 2 == c))
            def _():
                act(z_copy(p, d))

    def w1_arrive(p):
        for d in range(1, PLANES):
            @pl.when((y - d) % PLANES == p)
            def _():
                w1_copy(d).wait_recv()

        @pl.when(y == p)
        def _():
            w1_own().wait()

    def z_issue(p):
        z_sends(p, lambda copy: copy.start())

        @pl.when((zl == 1) | (c == 0))
        def _():
            shard_copy(p).start()

    def w1_to_z(p):
        w1_arrive(p)
        z_issue(p)

    def z_to_x(l):
        @pl.when((l % 2 == 1) | works)
        def _():
            for h in range(NZH):
                @pl.when((l % 2 != zl) | (zh != h))
                def _():
                    z_arrival(l, h).wait_recv()

            @pl.when(l % 2 == zl)
            def _():
                shard_copy(l // 2).wait()

            for i in range(2):
                x1_copy(l, i).start()

    def x1_to_x2(l):
        @pl.when((l % 2 == 1) | works)
        def _():
            for i in range(2):
                x1_copy(l, i).wait_recv()
                x2_copy(l, i).start()

            @pl.when(l % 2 == 0)
            def _():
                for d in (0, 1, 3):
                    for i in range(2):
                        p_copy(l, i, d).start()

            for d in (0, 1, 3):
                c_copy(l, d).start()

    def x2_to_c(l):
        @pl.when((l % 2 == 1) | works)
        def _():
            for i in range(2):
                x2_copy(l, i).wait_recv()

            @pl.when(l % 2 == 0)
            def _():
                for i in range(2):
                    p_copy(l, i, 2).start()

            c_copy(l, 2).start()

        @pl.when((l % 2 == 0) & jnp.logical_not(works))
        def _():
            for d in (0, 1, 3, 2):
                for i in range(2):
                    p_copy(l, i, d).wait_recv()
                c_copy(l, d).start()

    w1_arrive(0)

    @pl.when(zl == 0)
    def _():
        z_issue(0)

    @pl.when(y != 0)
    def _():
        for d in range(1, PLANES):
            w1_copy(d).start()

    for j in range(1, LAYERS):
        g_copy(j).start()
    z_to_x(0)

    @pl.when(zl == 1)
    def _():
        z_issue(0)

    x1_to_x2(0)
    z_to_x(1)
    w1_to_z(1)
    for u in range(2):
        for q in range(PLANES):
            frame_copy(u, q).wait()
    for j in range(1, LAYERS):
        g_copy(j).wait_recv()

    own_saved = LAYERS - 1 - sec
    pair_saved = LAYERS - 1 - pair[0]

    def out_at(ref, m, q):
        return ref.at[0, m, 0, :, pl.ds(q * QD, QD)]

    def own_save(l, u, q):
        return pltpu.make_async_copy(xs.at[l, u, q], out_at(out, 2 * zl + u, q), ol.at[u, q])

    def pair_save(l, u, q):
        return remote(xs.at[l, u, q], out_at(out, 2 * zl + u, q), os_.at[u, q], or_.at[u, q], pair)

    top = xs.at[LAYERS]

    def last_copy(u):
        return remote(
            top.at[u, y],
            out.at[0, 2 * zl + u, 0, :, pl.ds(pl.multiple_of(y * QD, QD), QD)],
            ls.at[u], lr.at[u, zl, y], (0, dp),
        )

    def far_half(u, i):
        half = top.at[u, 2, i * HF:(i + 1) * HF]
        return remote(half, half, hs.at[u, i], hr.at[u], (2 + 4 * i, dp))

    def far_whole(u):
        return remote(top.at[u, 2], top.at[u, 3], ls.at[u], fr.at[u], (2, dp))

    def near_whole(u):
        return remote(top.at[u, 1], top.at[u, 1], ls.at[u], fr.at[u], (1, dp))

    def half_on(u):
        i = y // 2
        part = pl.ds(pl.multiple_of(i * HF, HF), HF)
        return remote(
            top.at[u, 2, part], out.at[0, u, 0, part, 2 * QD:3 * QD], hs.at[u, 0], rr.at[u, i], (0, dp)
        )

    def far_on(u):
        return remote(top.at[u, 3], out_at(out, 2 + u, 2), hs.at[u, 1], lr.at[u, 1, 2], (0, dp))

    def near_on(u):
        return remote(top.at[u, 1], out_at(out, 2 + u, 1), hs.at[u, 1], lr.at[u, 1, 1], (0, dp))

    def half_arrival(u, i):
        return remote(
            top.at[u, 2, i * HF:(i + 1) * HF], out.at[0, u, 0, i * HF:(i + 1) * HF, 2 * QD:3 * QD],
            hs.at[u, 0], rr.at[u, i], (1, dp),
        )

    direct = (sec == 1) | (sec == 2) | (sec > 5)
    halves_on = (sec == 2) | (sec == 6)

    def last_own(u):
        return pltpu.make_async_copy(xs.at[LAYERS, u, 0], out_at(out, u, 0), ls.at[u])

    def last_arrival(u, zz, q):
        return remote(
            xs.at[LAYERS, u, q], out_at(out, 2 * zz + u, q), ls.at[u], lr.at[u, zz, q], (1, dp)
        )

    def saves(l, first, last):
        def due(saved):
            return (saved >= first) & (saved <= last) & (l == 6)

        for u in range(2):
            @pl.when(due(own_saved) | (own_saved == 6) & (first == 5) & (l == 7))
            def _():
                for q in range(PLANES):
                    own_save(own_saved + 1, u, q).start()

            @pl.when(due(pair_saved))
            def _():
                for q in range(PLANES):
                    pair_save(pair_saved + 1, u, q).start()

    def late_copy(u):
        return remote(
            xs.at[LAYERS - 1, u, y],
            out.at[0, 2 * zl + u, 0, :, pl.ds(pl.multiple_of(y * QD, QD), QD)],
            es.at[u], er.at[u, y], (1, dp),
        )

    def late_arrival(u, q):
        return remote(
            xs.at[LAYERS - 1, u, q], out_at(out, u, q), es.at[u], er.at[u, q], (0, dp)
        )

    rows = lax.broadcasted_iota(jnp.int32, (FR, FR), 0)
    cols = lax.broadcasted_iota(jnp.int32, (FR, FR), 1)
    keep = (cols < rows) | ((rows == 0) & (cols == 0))

    def compute(l, u):
        parts = [xs[l, u, q].astype(F32) for q in range(PLANES)]
        square = sum(jnp.sum(p * p, axis=-1, keepdims=True) for p in parts)
        scale = lax.rsqrt(square * (1.0 / D) + 1e-05)
        for q in range(PLANES):
            nrm[q] = (parts[q] * scale * gt[l, 0:1, q * QD:(q + 1) * QD]).astype(BF16)
        lhs = jnp.concatenate([nrm[q] for q in range(PLANES)], axis=1)
        proj = jnp.dot(lhs, w[l].reshape(D, QD), preferred_element_type=F32).astype(BF16)
        values = nrm[y]
        temper = gt[l, 1:2, pl.ds(pl.multiple_of(y * QD, QD), QD)]
        heads = [proj[:, k * HEAD:(k + 1) * HEAD] for k in range(QH)]
        scores = [
            lax.dot_general(h, h, (((1,), (1,)), ((), ())), preferred_element_type=F32) for h in heads
        ]
        scores = [
            jnp.where(keep, s * temper[:, k * HEAD:(k + 1) * HEAD], -1e30) for k, s in enumerate(scores)
        ]
        tops = [jnp.max(s, axis=-1, keepdims=True) for s in scores]
        expo = [jnp.exp(s - t) for s, t in zip(scores, tops)]
        sums = [jnp.sum(e, axis=-1, keepdims=True) for e in expo]
        weights = [(e / s).astype(BF16) for e, s in zip(expo, sums)]
        mixed = [
            jnp.dot(wt, values[:, k * HEAD:(k + 1) * HEAD], preferred_element_type=F32)
            for k, wt in enumerate(weights)
        ]
        xs[l + 1, u, y] = (xs[l, u, y].astype(F32) + jnp.concatenate(mixed, axis=1)).astype(BF16)

    def state_in(l, u):
        @pl.when(l > 0)
        def _():
            for i in range(2):
                y1_copy(l, u, i).wait_recv()
                y2_copy(l, u, i).start()

    def step(l, u):
        @pl.when(l > 0)
        def _():
            for i in range(2):
                y2_copy(l, u, i).wait_recv()

        compute(l, u)

        @pl.when((l == LAYERS - 1) & (sec == 0))
        def _():
            last_own(u).start()

        @pl.when((l == LAYERS - 1) & direct)
        def _():
            last_copy(u).start()

        @pl.when((l == LAYERS - 1) & (sec == 4))
        def _():
            for i in range(2):
                far_half(u, i).start()

        @pl.when((l == LAYERS - 1) & (sec == 5))
        def _():
            far_whole(u).start()

        @pl.when((l == LAYERS - 1) & (sec == 3))
        def _():
            near_whole(u).start()

        @pl.when(l + 1 < LAYERS)
        def _():
            for i in range(2):
                y1_copy(l + 1, u, i).start()

    def ahead(l):
        @pl.when(l + 2 < LAYERS)
        def _():
            z_to_x(l + 2)

        for p in (2, 3):
            @pl.when(l + 2 == 2 * p - 2)
            def _():
                w1_to_z(p)

    def layer(l, carry):
        x2_to_c(l)
        saves(l, 0, 4)
        state_in(l, 0)

        @pl.when((l > 0) & (l + 1 < LAYERS))
        def _():
            x1_to_x2(l + 1)

        state_in(l, 1)
        for d in range(NX):
            c_copy(l, d).wait_recv()
        step(l, 0)

        @pl.when(l == 0)
        def _():
            x1_to_x2(1)

        ahead(l)

        @pl.when((l == LAYERS - 1) & (zl == 0))
        def _():
            for u in range(2):
                late_copy(u).start()

        step(l, 1)
        saves(l, 5, 5)
        return carry

    lax.fori_loop(0, LAYERS, layer, 0)

    for u in range(2):
        @pl.when(halves_on)
        def _():
            far_half(u, 0).wait_recv()
            half_on(u).start()

        @pl.when(sec == 2)
        def _():
            far_whole(u).wait_recv()
            far_on(u).start()

        @pl.when(sec == 1)
        def _():
            near_whole(u).wait_recv()
            near_on(u).start()

    for d in range(1, PLANES):
        w1_copy(d).wait_send()
    for j in range(1, LAYERS):
        g_copy(j).wait_send()
    for p in range(4):
        z_sends(p, lambda copy: copy.wait_send())

    def drain(l, carry):
        @pl.when((l % 2 == 1) | works)
        def _():
            for i in range(2):
                x1_copy(l, i).wait_send()
                x2_copy(l, i).wait_send()

        @pl.when((l % 2 == 0) & works)
        def _():
            for i in range(2):
                for d in range(NX):
                    p_copy(l, i, d).wait_send()

        for d in range(NX):
            c_copy(l, d).wait_send()

        @pl.when(l > 0)
        def _():
            for u in range(2):
                for i in range(2):
                    y1_copy(l, u, i).wait_send()
                    y2_copy(l, u, i).wait_send()

        return carry

    lax.fori_loop(0, LAYERS, drain, 0)

    @pl.when(sec != 0)
    def _():
        for u in range(2):
            for q in range(PLANES):
                own_save(0, u, q).wait()

    @pl.when(direct)
    def _():
        for u in range(2):
            last_copy(u).wait_send()

    @pl.when(sec == 4)
    def _():
        for u in range(2):
            for i in range(2):
                far_half(u, i).wait_send()

    @pl.when(sec == 5)
    def _():
        for u in range(2):
            far_whole(u).wait_send()

    @pl.when(sec == 3)
    def _():
        for u in range(2):
            near_whole(u).wait_send()

    @pl.when(sec == 2)
    def _():
        for u in range(2):
            far_on(u).wait_send()

    @pl.when(halves_on)
    def _():
        for u in range(2):
            half_on(u).wait_send()

    @pl.when(sec == 1)
    def _():
        for u in range(2):
            near_on(u).wait_send()

    @pl.when(sec > 1)
    def _():
        for u in range(2):
            for q in range(PLANES):
                pair_save(0, u, q).wait_send()
                pair_save(0, u, q).wait_recv()

    @pl.when(zl == 0)
    def _():
        for u in range(2):
            late_copy(u).wait_send()

    @pl.when(sec == 1)
    def _():
        for u in range(2):
            for q in range(PLANES):
                late_arrival(u, q).wait_recv()

    @pl.when(sec == 0)
    def _():
        for u in range(2):
            last_own(u).wait()
            for zz in range(2):
                for q in range(PLANES):
                    if (zz, q) not in ((0, 0), (0, 2)):
                        last_arrival(u, zz, q).wait_recv()
            for i in range(2):
                half_arrival(u, i).wait_recv()


def local(frames, gains, w_shared, temper):
    dma = pltpu.SemaphoreType.DMA
    any_space = pl.BlockSpec(memory_space=pl.ANY)
    return pl.pallas_call(
        kernel,
        out_shape=jax.ShapeDtypeStruct((1,) + frames.shape, BF16),
        in_specs=[any_space, any_space] + [pl.BlockSpec(memory_space=pltpu.VMEM)] * 2,
        out_specs=any_space,
        scratch_shapes=[
            pltpu.VMEM((LAYERS, NZH, NX, 2, ROWS, QD), BF16),
            pltpu.VMEM((PLANES, ROWS, QD), BF16),
            pltpu.VMEM((LAYERS + 1, 2, PLANES, FR, QD), BF16),
            pltpu.VMEM((PLANES, FR, QD), BF16),
            pltpu.VMEM((LAYERS, 2, D), F32),
            dma((4,)), dma((3,)), dma((4,)),
            dma((4, 7)), dma((LAYERS, NZH)),
            dma((LAYERS, 2)), dma((LAYERS, 2)),
            dma((LAYERS, 2)), dma((LAYERS, 2)),
            dma((LAYERS // 2, 2, NX)), dma((LAYERS // 2, 2, NX)),
            dma((LAYERS, 4)), dma((LAYERS, 4)),
            dma((LAYERS, 2, 2)), dma((LAYERS, 2, 2)),
            dma((LAYERS, 2, 2)), dma((LAYERS, 2, 2)),
            dma((LAYERS - 1,)), dma((LAYERS - 1,)),
            dma((2, PLANES)), dma((2, PLANES)),
            dma((2, PLANES)), dma((2, PLANES)),
            dma((2,)), dma((2, 2, PLANES)),
            dma((2,)), dma((2, PLANES)),
            dma((2, 2)), dma((2,)), dma((2, 2)), dma((2,)),
        ],
        compiler_params=pltpu.CompilerParams(
            collective_id=0, has_side_effects=True, vmem_limit_bytes=58 << 20
        ),
    )(frames, w_shared, gains, temper)


def solution(mesh):
    in_specs = (
        P(None, "dp", None, None),
        P("section", None),
        P("section", "dp", None),
        P("section", None),
    )
    out_specs = P("section", None, "dp", None, None)
    return jax.shard_map(local, mesh=mesh, in_specs=in_specs, out_specs=out_specs, check_vma=False)
```

```python
import functools

import jax
import jax.numpy as jnp
from jax import lax
from jax.experimental import pallas as pl
from jax.experimental.pallas import tpu as pltpu
from jax.sharding import PartitionSpec as P

MESH = pl.DeviceIdType.MESH
F32 = jnp.float32
BF16 = jnp.bfloat16

D = 2560
FR = 128
HF = FR // 2
LAYERS = 8
PLANES = 4
QD = D // PLANES
HEAD = 128
QH = QD // HEAD
NX = 4
NZH = 4
ROWS = 80


def kernel(
    frames, w_in, gains, temper_in, out,
    w, shard, xs, nrm, gt,
    w1s, w1r, sl, zs, zr, x1s, x1r, x2s, x2r, ps, pr, cs, cr, y1s, y1r, y2s, y2r, gs, gr, fl, ol, os_, or_, ls, lr, es, er, hs, hr, rr, fr,
):
    sec = lax.axis_index("section")
    dp = lax.axis_index("dp")
    y = sec // 2
    zl = sec % 2
    zh = dp // 8
    x = (dp // 2) % NX
    c = dp % 2
    z = zh * 2 + zl

    def at_y(q):
        return (q * 2 + zl, dp)

    def at_x(xx):
        return (sec, zh * 8 + xx * 2 + c)

    def at_z(zz):
        return (y * 2 + zz % 2, (zz // 2) * 8 + x * 2 + c)

    sibling = (sec, zh * 8 + x * 2 + 1 - c)
    pair = (y * 2 + 1 - zl, dp)

    peers = [at_y((y + d) % PLANES) for d in range(1, PLANES)]
    peers += [at_x((x + 1) % NX), at_x((x + 3) % NX)]
    peers += [at_z((z + d) % 8) for d in range(1, 8)]
    peers += [sibling]
    peers += [(((y + d) % PLANES) * 2 + 1 - zl, dp) for d in range(1, PLANES)]
    barrier = pltpu.get_barrier_semaphore()
    for p in peers:
        pl.semaphore_signal(barrier, inc=1, device_id=p, device_id_type=MESH)
    pl.semaphore_wait(barrier, len(peers))

    def remote(src, dst, s, r, to):
        return pltpu.make_async_remote_copy(
            src_ref=src, dst_ref=dst, send_sem=s, recv_sem=r, device_id=to, device_id_type=MESH
        )

    def w1_copy(d):
        q = (y + d) % PLANES
        return remote(
            w_in.at[0, :, pl.ds(pl.multiple_of(q * QD, QD), QD)],
            shard.at[y],
            w1s.at[d - 1], w1r.at[d - 1], at_y(q),
        )

    def w1_own():
        return pltpu.make_async_copy(
            w_in.at[0, :, pl.ds(pl.multiple_of(y * QD, QD), QD)], shard.at[y], w1s.at[3]
        )

    def shard_copy(p):
        return pltpu.make_async_copy(shard.at[p], w.at[2 * p + zl, zh, x, c], sl.at[p])

    def z_copy(p, d):
        l = 2 * p + zl
        return remote(
            shard.at[p], w.at[l, zh, x, c], zs.at[p, d - 1], zr.at[l, zh], at_z((z + d) % 8)
        )

    def z_arrival(l, h):
        return remote(w.at[l, h, x, c], w.at[l, h, x, c], zs.at[0, 0], zr.at[l, h], pair)

    def x1_copy(l, i):
        return remote(
            w.at[l, :, x, c], w.at[l, :, x, c], x1s.at[l, i], x1r.at[l, i], at_x((x + 1 + 2 * i) % NX)
        )

    def x2_copy(l, i):
        half = w.at[l, 2 * i:2 * i + 2, (x + 3 - 2 * i) % NX, c]
        return remote(half, half, x2s.at[l, i], x2r.at[l, i], at_x((x + 1 + 2 * i) % NX))

    def p_copy(l, i, d):
        part = w.at[l, 2 * i:2 * i + 2, (x + d) % NX, c]
        return remote(
            part, part, ps.at[l // 2, i, d], pr.at[l // 2, i, d], at_z((z + 1 + 6 * i) % 8)
        )

    def c_copy(l, d):
        xx = (x + d) % NX
        return remote(w.at[l, :, xx, c], w.at[l, :, xx, c], cs.at[l, d], cr.at[l, d], sibling)

    def y1_copy(l, u, i, k):
        h = i if k == 0 else 1 - i
        part = xs.at[l, u, y, h * HF:(h + 1) * HF]
        return remote(
            part, part, y1s.at[l - 1, u, i, k], y1r.at[l - 1, u, i, k], at_y((y + 1 + 2 * i) % PLANES)
        )

    def y2_copy(l, u, i):
        half = xs.at[l, u, (y + 3 - 2 * i) % PLANES, i * HF:(i + 1) * HF]
        return remote(
            half, half, y2s.at[l - 1, u, i], y2r.at[l - 1, u, i], at_y((y + 1 + 2 * i) % PLANES)
        )

    def g_copy(j):
        s = (sec + j) % LAYERS
        return remote(gt.at[sec], gt.at[sec], gs.at[j - 1], gr.at[j - 1], (s, dp))

    def frame_copy(u, q):
        return pltpu.make_async_copy(
            frames.at[2 * zl + u, 0, :, pl.ds(q * QD, QD)], xs.at[0, u, q], fl.at[u, q]
        )

    w1_own().start()

    @pl.when(y == 0)
    def _():
        for d in range(1, PLANES):
            w1_copy(d).start()

    for u in range(2):
        for q in range(PLANES):
            frame_copy(u, q).start()
    gt[sec, 0:1] = gains[...]
    tempers = temper_in[...] / (HEAD ** 0.5)
    for k in range(D // HEAD):
        gt[sec, 1:2, k * HEAD:(k + 1) * HEAD] = jnp.broadcast_to(tempers[:, k:k + 1], (1, HEAD))

    works = zl == c

    def z_sends(p, act):
        for d in range(1, 8):
            @pl.when((zl == 1) | (d % 2 == c))
            def _():
                act(z_copy(p, d))

    def w1_arrive(p):
        for d in range(1, PLANES):
            @pl.when((y - d) % PLANES == p)
            def _():
                w1_copy(d).wait_recv()

        @pl.when(y == p)
        def _():
            w1_own().wait()

    def z_issue(p):
        z_sends(p, lambda copy: copy.start())

        @pl.when((zl == 1) | (c == 0))
        def _():
            shard_copy(p).start()

    def w1_to_z(p):
        w1_arrive(p)
        z_issue(p)

    def z_to_x(l):
        @pl.when((l % 2 == 1) | works)
        def _():
            for h in range(NZH):
                @pl.when((l % 2 != zl) | (zh != h))
                def _():
                    z_arrival(l, h).wait_recv()

            @pl.when(l % 2 == zl)
            def _():
                shard_copy(l // 2).wait()

            for i in range(2):
                x1_copy(l, i).start()

    def x1_to_x2(l):
        @pl.when((l % 2 == 1) | works)
        def _():
            for i in range(2):
                x1_copy(l, i).wait_recv()
                x2_copy(l, i).start()

            @pl.when(l % 2 == 0)
            def _():
                for d in (0, 1, 3):
                    for i in range(2):
                        p_copy(l, i, d).start()

            for d in (0, 1, 3):
                c_copy(l, d).start()

    def x2_to_c(l):
        @pl.when((l % 2 == 1) | works)
        def _():
            for i in range(2):
                x2_copy(l, i).wait_recv()

            @pl.when(l % 2 == 0)
            def _():
                for i in range(2):
                    p_copy(l, i, 2).start()

            c_copy(l, 2).start()

        @pl.when((l % 2 == 0) & jnp.logical_not(works))
        def _():
            for d in (0, 1, 3, 2):
                for i in range(2):
                    p_copy(l, i, d).wait_recv()
                c_copy(l, d).start()

    w1_arrive(0)

    @pl.when(zl == 0)
    def _():
        z_issue(0)

    @pl.when(y != 0)
    def _():
        for d in range(1, PLANES):
            w1_copy(d).start()

    for j in range(1, LAYERS):
        g_copy(j).start()
    z_to_x(0)

    @pl.when(zl == 1)
    def _():
        z_issue(0)

    x1_to_x2(0)
    z_to_x(1)
    w1_to_z(1)
    for u in range(2):
        for q in range(PLANES):
            frame_copy(u, q).wait()
    for j in range(1, LAYERS):
        g_copy(j).wait_recv()

    own_saved = LAYERS - 1 - sec
    pair_saved = LAYERS - 1 - pair[0]

    def out_at(ref, m, q):
        return ref.at[0, m, 0, :, pl.ds(q * QD, QD)]

    def own_save(l, u, q):
        return pltpu.make_async_copy(xs.at[l, u, q], out_at(out, 2 * zl + u, q), ol.at[u, q])

    def pair_save(l, u, q):
        return remote(xs.at[l, u, q], out_at(out, 2 * zl + u, q), os_.at[u, q], or_.at[u, q], pair)

    top = xs.at[LAYERS]

    def last_copy(u):
        return remote(
            top.at[u, y],
            out.at[0, 2 * zl + u, 0, :, pl.ds(pl.multiple_of(y * QD, QD), QD)],
            ls.at[u], lr.at[u, zl, y], (0, dp),
        )

    def far_half(u, i):
        half = top.at[u, 2, i * HF:(i + 1) * HF]
        return remote(half, half, hs.at[u, i], hr.at[u], (2 + 4 * i, dp))

    def far_whole(u):
        return remote(top.at[u, 2], top.at[u, 3], ls.at[u], fr.at[u], (2, dp))

    def near_whole(u):
        return remote(top.at[u, 1], top.at[u, 1], ls.at[u], fr.at[u], (1, dp))

    def half_on(u):
        i = y // 2
        part = pl.ds(pl.multiple_of(i * HF, HF), HF)
        return remote(
            top.at[u, 2, part], out.at[0, u, 0, part, 2 * QD:3 * QD], hs.at[u, 0], rr.at[u, i], (0, dp)
        )

    def far_on(u):
        return remote(top.at[u, 3], out_at(out, 2 + u, 2), hs.at[u, 1], lr.at[u, 1, 2], (0, dp))

    def near_on(u):
        return remote(top.at[u, 1], out_at(out, 2 + u, 1), hs.at[u, 1], lr.at[u, 1, 1], (0, dp))

    def half_arrival(u, i):
        return remote(
            top.at[u, 2, i * HF:(i + 1) * HF], out.at[0, u, 0, i * HF:(i + 1) * HF, 2 * QD:3 * QD],
            hs.at[u, 0], rr.at[u, i], (1, dp),
        )

    direct = (sec == 1) | (sec == 2) | (sec > 5)
    halves_on = (sec == 2) | (sec == 6)

    def last_own(u):
        return pltpu.make_async_copy(xs.at[LAYERS, u, 0], out_at(out, u, 0), ls.at[u])

    def last_arrival(u, zz, q):
        return remote(
            xs.at[LAYERS, u, q], out_at(out, 2 * zz + u, q), ls.at[u], lr.at[u, zz, q], (1, dp)
        )

    def saves(l, first, last):
        def due(saved):
            return (saved >= first) & (saved <= last) & (l == 6)

        for u in range(2):
            @pl.when(due(own_saved) | (own_saved == 6) & (first == 5) & (l == 7))
            def _():
                for q in range(PLANES):
                    own_save(own_saved + 1, u, q).start()

            @pl.when(due(pair_saved))
            def _():
                for q in range(PLANES):
                    pair_save(pair_saved + 1, u, q).start()

    def late_copy(u):
        return remote(
            xs.at[LAYERS - 1, u, y],
            out.at[0, 2 * zl + u, 0, :, pl.ds(pl.multiple_of(y * QD, QD), QD)],
            es.at[u], er.at[u, y], (1, dp),
        )

    def late_arrival(u, q):
        return remote(
            xs.at[LAYERS - 1, u, q], out_at(out, u, q), es.at[u], er.at[u, q], (0, dp)
        )

    rows = lax.broadcasted_iota(jnp.int32, (FR, FR), 0)
    cols = lax.broadcasted_iota(jnp.int32, (FR, FR), 1)
    keep = (cols < rows) | ((rows == 0) & (cols == 0))

    def compute(l, u):
        parts = [xs[l, u, q].astype(F32) for q in range(PLANES)]
        square = sum(jnp.sum(p * p, axis=-1, keepdims=True) for p in parts)
        scale = lax.rsqrt(square * (1.0 / D) + 1e-05)
        for q in range(PLANES):
            nrm[q] = (parts[q] * scale * gt[l, 0:1, q * QD:(q + 1) * QD]).astype(BF16)
        lhs = jnp.concatenate([nrm[q] for q in range(PLANES)], axis=1)
        proj = jnp.dot(lhs, w[l].reshape(D, QD), preferred_element_type=F32).astype(BF16)
        values = nrm[y]
        temper = gt[l, 1:2, pl.ds(pl.multiple_of(y * QD, QD), QD)]
        heads = [proj[:, k * HEAD:(k + 1) * HEAD] for k in range(QH)]
        scores = [
            lax.dot_general(h, h, (((1,), (1,)), ((), ())), preferred_element_type=F32) for h in heads
        ]
        scores = [
            jnp.where(keep, s * temper[:, k * HEAD:(k + 1) * HEAD], -1e30) for k, s in enumerate(scores)
        ]
        tops = [jnp.max(s, axis=-1, keepdims=True) for s in scores]
        expo = [jnp.exp(s - t) for s, t in zip(scores, tops)]
        sums = [jnp.sum(e, axis=-1, keepdims=True) for e in expo]
        weights = [(e / s).astype(BF16) for e, s in zip(expo, sums)]
        mixed = [
            jnp.dot(wt, values[:, k * HEAD:(k + 1) * HEAD], preferred_element_type=F32)
            for k, wt in enumerate(weights)
        ]
        xs[l + 1, u, y] = (xs[l, u, y].astype(F32) + jnp.concatenate(mixed, axis=1)).astype(BF16)

    def state_in(l, u):
        @pl.when(l > 0)
        def _():
            for i in range(2):
                y1_copy(l, u, i, 0).wait_recv()
                y2_copy(l, u, i).start()

    def step(l, u):
        @pl.when(l > 0)
        def _():
            for i in range(2):
                y1_copy(l, u, i, 1).wait_recv()
                y2_copy(l, u, i).wait_recv()

        compute(l, u)

        @pl.when((l == LAYERS - 1) & (sec == 0))
        def _():
            last_own(u).start()

        @pl.when((l == LAYERS - 1) & direct)
        def _():
            last_copy(u).start()

        @pl.when((l == LAYERS - 1) & (sec == 4))
        def _():
            for i in range(2):
                far_half(u, i).start()

        @pl.when((l == LAYERS - 1) & (sec == 5))
        def _():
            far_whole(u).start()

        @pl.when((l == LAYERS - 1) & (sec == 3))
        def _():
            near_whole(u).start()

        @pl.when(l + 1 < LAYERS)
        def _():
            for i in range(2):
                y1_copy(l + 1, u, i, 0).start()
            if u == 1:
                for v in range(2):
                    for i in range(2):
                        y1_copy(l + 1, v, i, 1).start()

    def ahead(l):
        @pl.when(l + 2 < LAYERS)
        def _():
            z_to_x(l + 2)

        for p in (2, 3):
            @pl.when(l + 2 == 2 * p - 2)
            def _():
                w1_to_z(p)

    def layer(l, carry):
        x2_to_c(l)
        saves(l, 0, 4)
        state_in(l, 0)

        @pl.when((l > 0) & (l + 1 < LAYERS))
        def _():
            x1_to_x2(l + 1)

        state_in(l, 1)
        for d in range(NX):
            c_copy(l, d).wait_recv()

        @pl.when((l == LAYERS - 1) & (zl == 0))
        def _():
            for u in range(2):
                late_copy(u).start()

        step(l, 0)

        @pl.when(l == 0)
        def _():
            x1_to_x2(1)

        ahead(l)

        step(l, 1)
        saves(l, 5, 5)
        return carry

    lax.fori_loop(0, LAYERS, layer, 0)

    for u in range(2):
        @pl.when(halves_on)
        def _():
            far_half(u, 0).wait_recv()
            half_on(u).start()

        @pl.when(sec == 2)
        def _():
            far_whole(u).wait_recv()
            far_on(u).start()

        @pl.when(sec == 1)
        def _():
            near_whole(u).wait_recv()
            near_on(u).start()

    for d in range(1, PLANES):
        w1_copy(d).wait_send()
    for j in range(1, LAYERS):
        g_copy(j).wait_send()
    for p in range(4):
        z_sends(p, lambda copy: copy.wait_send())

    def drain(l, carry):
        @pl.when((l % 2 == 1) | works)
        def _():
            for i in range(2):
                x1_copy(l, i).wait_send()
                x2_copy(l, i).wait_send()

        @pl.when((l % 2 == 0) & works)
        def _():
            for i in range(2):
                for d in range(NX):
                    p_copy(l, i, d).wait_send()

        for d in range(NX):
            c_copy(l, d).wait_send()

        @pl.when(l > 0)
        def _():
            for u in range(2):
                for i in range(2):
                    for k in range(2):
                        y1_copy(l, u, i, k).wait_send()
                    y2_copy(l, u, i).wait_send()

        return carry

    lax.fori_loop(0, LAYERS, drain, 0)

    @pl.when(sec != 0)
    def _():
        for u in range(2):
            for q in range(PLANES):
                own_save(0, u, q).wait()

    @pl.when(direct)
    def _():
        for u in range(2):
            last_copy(u).wait_send()

    @pl.when(sec == 4)
    def _():
        for u in range(2):
            for i in range(2):
                far_half(u, i).wait_send()

    @pl.when(sec == 5)
    def _():
        for u in range(2):
            far_whole(u).wait_send()

    @pl.when(sec == 3)
    def _():
        for u in range(2):
            near_whole(u).wait_send()

    @pl.when(sec == 2)
    def _():
        for u in range(2):
            far_on(u).wait_send()

    @pl.when(halves_on)
    def _():
        for u in range(2):
            half_on(u).wait_send()

    @pl.when(sec == 1)
    def _():
        for u in range(2):
            near_on(u).wait_send()

    @pl.when(sec > 1)
    def _():
        for u in range(2):
            for q in range(PLANES):
                pair_save(0, u, q).wait_send()
                pair_save(0, u, q).wait_recv()

    @pl.when(zl == 0)
    def _():
        for u in range(2):
            late_copy(u).wait_send()

    @pl.when(sec == 1)
    def _():
        for u in range(2):
            for q in range(PLANES):
                late_arrival(u, q).wait_recv()

    @pl.when(sec == 0)
    def _():
        for u in range(2):
            last_own(u).wait()
            for zz in range(2):
                for q in range(PLANES):
                    if (zz, q) not in ((0, 0), (0, 2)):
                        last_arrival(u, zz, q).wait_recv()
            for i in range(2):
                half_arrival(u, i).wait_recv()


def local(frames, gains, w_shared, temper):
    dma = pltpu.SemaphoreType.DMA
    any_space = pl.BlockSpec(memory_space=pl.ANY)
    return pl.pallas_call(
        kernel,
        out_shape=jax.ShapeDtypeStruct((1,) + frames.shape, BF16),
        in_specs=[any_space, any_space] + [pl.BlockSpec(memory_space=pltpu.VMEM)] * 2,
        out_specs=any_space,
        scratch_shapes=[
            pltpu.VMEM((LAYERS, NZH, NX, 2, ROWS, QD), BF16),
            pltpu.VMEM((PLANES, ROWS, QD), BF16),
            pltpu.VMEM((LAYERS + 1, 2, PLANES, FR, QD), BF16),
            pltpu.VMEM((PLANES, FR, QD), BF16),
            pltpu.VMEM((LAYERS, 2, D), F32),
            dma((4,)), dma((3,)), dma((4,)),
            dma((4, 7)), dma((LAYERS, NZH)),
            dma((LAYERS, 2)), dma((LAYERS, 2)),
            dma((LAYERS, 2)), dma((LAYERS, 2)),
            dma((LAYERS // 2, 2, NX)), dma((LAYERS // 2, 2, NX)),
            dma((LAYERS, 4)), dma((LAYERS, 4)),
            dma((LAYERS, 2, 2, 2)), dma((LAYERS, 2, 2, 2)),
            dma((LAYERS, 2, 2)), dma((LAYERS, 2, 2)),
            dma((LAYERS - 1,)), dma((LAYERS - 1,)),
            dma((2, PLANES)), dma((2, PLANES)),
            dma((2, PLANES)), dma((2, PLANES)),
            dma((2,)), dma((2, 2, PLANES)),
            dma((2,)), dma((2, PLANES)),
            dma((2, 2)), dma((2,)), dma((2, 2)), dma((2,)),
        ],
        compiler_params=pltpu.CompilerParams(
            collective_id=0, has_side_effects=True, vmem_limit_bytes=58 << 20
        ),
    )(frames, w_shared, gains, temper)


def solution(mesh):
    in_specs = (
        P(None, "dp", None, None),
        P("section", None),
        P("section", "dp", None),
        P("section", None),
    )
    out_specs = P("section", None, "dp", None, None)
    return jax.shard_map(local, mesh=mesh, in_specs=in_specs, out_specs=out_specs, check_vma=False)
```

```python
import functools

import jax
import jax.numpy as jnp
from jax import lax
from jax.experimental import pallas as pl
from jax.experimental.pallas import tpu as pltpu
from jax.sharding import PartitionSpec as P

MESH = pl.DeviceIdType.MESH
F32 = jnp.float32
BF16 = jnp.bfloat16

D = 2560
FR = 128
HF = FR // 2
LAYERS = 8
PLANES = 4
QD = D // PLANES
HEAD = 128
QH = QD // HEAD
NX = 4
NZH = 4
ROWS = 80


def kernel(
    frames, w_in, gains, temper_in, out,
    w, shard, xs, nrm, gt,
    w1s, w1r, sl, zs, zr, x1s, x1r, x2s, x2r, ps, pr, cs, cr, y1s, y1r, y2s, y2r, gs, gr, fl, ol, os_, or_, ls, lr, es, er, hs, hr, rr, fr,
):
    sec = lax.axis_index("section")
    dp = lax.axis_index("dp")
    y = sec // 2
    zl = sec % 2
    zh = dp // 8
    x = (dp // 2) % NX
    c = dp % 2
    z = zh * 2 + zl

    def at_y(q):
        return (q * 2 + zl, dp)

    def at_x(xx):
        return (sec, zh * 8 + xx * 2 + c)

    def at_z(zz):
        return (y * 2 + zz % 2, (zz // 2) * 8 + x * 2 + c)

    sibling = (sec, zh * 8 + x * 2 + 1 - c)
    pair = (y * 2 + 1 - zl, dp)

    peers = [at_y((y + d) % PLANES) for d in range(1, PLANES)]
    peers += [at_x((x + 1) % NX), at_x((x + 3) % NX)]
    peers += [at_z((z + d) % 8) for d in range(1, 8)]
    peers += [sibling]
    peers += [(((y + d) % PLANES) * 2 + 1 - zl, dp) for d in range(1, PLANES)]
    barrier = pltpu.get_barrier_semaphore()
    for p in peers:
        pl.semaphore_signal(barrier, inc=1, device_id=p, device_id_type=MESH)
    pl.semaphore_wait(barrier, len(peers))

    def remote(src, dst, s, r, to):
        return pltpu.make_async_remote_copy(
            src_ref=src, dst_ref=dst, send_sem=s, recv_sem=r, device_id=to, device_id_type=MESH
        )

    def w1_copy(d):
        q = (y + d) % PLANES
        return remote(
            w_in.at[0, :, pl.ds(pl.multiple_of(q * QD, QD), QD)],
            shard.at[y],
            w1s.at[d - 1], w1r.at[d - 1], at_y(q),
        )

    def w1_own():
        return pltpu.make_async_copy(
            w_in.at[0, :, pl.ds(pl.multiple_of(y * QD, QD), QD)], shard.at[y], w1s.at[3]
        )

    def shard_copy(p):
        return pltpu.make_async_copy(shard.at[p], w.at[2 * p + zl, zh, x, c], sl.at[p])

    def z_copy(p, d):
        l = 2 * p + zl
        return remote(
            shard.at[p], w.at[l, zh, x, c], zs.at[p, d - 1], zr.at[l, zh], at_z((z + d) % 8)
        )

    def z_arrival(l, h):
        return remote(w.at[l, h, x, c], w.at[l, h, x, c], zs.at[0, 0], zr.at[l, h], pair)

    def x1_copy(l, i):
        return remote(
            w.at[l, :, x, c], w.at[l, :, x, c], x1s.at[l, i], x1r.at[l, i], at_x((x + 1 + 2 * i) % NX)
        )

    def x2_copy(l, i):
        half = w.at[l, 2 * i:2 * i + 2, (x + 3 - 2 * i) % NX, c]
        return remote(half, half, x2s.at[l, i], x2r.at[l, i], at_x((x + 1 + 2 * i) % NX))

    def p_copy(l, i, d):
        part = w.at[l, 2 * i:2 * i + 2, (x + d) % NX, c]
        return remote(
            part, part, ps.at[l // 2, i, d], pr.at[l // 2, i, d], at_z((z + 1 + 6 * i) % 8)
        )

    def c_copy(l, d):
        xx = (x + d) % NX
        return remote(w.at[l, :, xx, c], w.at[l, :, xx, c], cs.at[l, d], cr.at[l, d], sibling)

    def y1_copy(l, u, i):
        return remote(
            xs.at[l, u, y], xs.at[l, u, y], y1s.at[l - 1, u, i], y1r.at[l - 1, u, i],
            at_y((y + 1 + 2 * i) % PLANES),
        )

    def y2_copy(l, u, i):
        half = xs.at[l, u, (y + 3 - 2 * i) % PLANES, i * HF:(i + 1) * HF]
        return remote(
            half, half, y2s.at[l - 1, u, i], y2r.at[l - 1, u, i], at_y((y + 1 + 2 * i) % PLANES)
        )

    def g_copy(j):
        s = (sec + j) % LAYERS
        return remote(gt.at[sec], gt.at[sec], gs.at[j - 1], gr.at[j - 1], (s, dp))

    def frame_copy(u, q):
        return pltpu.make_async_copy(
            frames.at[2 * zl + u, 0, :, pl.ds(q * QD, QD)], xs.at[0, u, q], fl.at[u, q]
        )

    w1_own().start()

    @pl.when(y == 0)
    def _():
        for d in range(1, PLANES):
            w1_copy(d).start()

    for u in range(2):
        for q in range(PLANES):
            frame_copy(u, q).start()
    gt[sec, 0:1] = gains[...]
    tempers = temper_in[...] / (HEAD ** 0.5)
    for k in range(D // HEAD):
        gt[sec, 1:2, k * HEAD:(k + 1) * HEAD] = jnp.broadcast_to(tempers[:, k:k + 1], (1, HEAD))

    works = zl == c

    def z_sends(p, act):
        for d in range(1, 8):
            @pl.when((zl == 1) | (d % 2 == c))
            def _():
                act(z_copy(p, d))

    def w1_arrive(p):
        for d in range(1, PLANES):
            @pl.when((y - d) % PLANES == p)
            def _():
                w1_copy(d).wait_recv()

        @pl.when(y == p)
        def _():
            w1_own().wait()

    def z_issue(p):
        z_sends(p, lambda copy: copy.start())

        @pl.when((zl == 1) | (c == 0))
        def _():
            shard_copy(p).start()

    def w1_to_z(p):
        w1_arrive(p)
        z_issue(p)

    def z_to_x(l):
        @pl.when((l % 2 == 1) | works)
        def _():
            for h in range(NZH):
                @pl.when((l % 2 != zl) | (zh != h))
                def _():
                    z_arrival(l, h).wait_recv()

            @pl.when(l % 2 == zl)
            def _():
                shard_copy(l // 2).wait()

            for i in range(2):
                x1_copy(l, i).start()

    def x1_to_x2(l):
        @pl.when((l % 2 == 1) | works)
        def _():
            for i in range(2):
                x1_copy(l, i).wait_recv()
                x2_copy(l, i).start()

            @pl.when(l % 2 == 0)
            def _():
                for d in (0, 1, 3):
                    for i in range(2):
                        p_copy(l, i, d).start()

            for d in (0, 1, 3):
                c_copy(l, d).start()

    def x2_to_c(l):
        @pl.when((l % 2 == 1) | works)
        def _():
            for i in range(2):
                x2_copy(l, i).wait_recv()

            @pl.when(l % 2 == 0)
            def _():
                for i in range(2):
                    p_copy(l, i, 2).start()

            c_copy(l, 2).start()

        @pl.when((l % 2 == 0) & jnp.logical_not(works))
        def _():
            for d in (0, 1, 3, 2):
                for i in range(2):
                    p_copy(l, i, d).wait_recv()
                c_copy(l, d).start()

    w1_arrive(0)

    @pl.when(zl == 0)
    def _():
        z_issue(0)

    @pl.when(y != 0)
    def _():
        for d in range(1, PLANES):
            w1_copy(d).start()

    for j in range(1, LAYERS):
        g_copy(j).start()
    z_to_x(0)

    @pl.when(zl == 1)
    def _():
        z_issue(0)

    x1_to_x2(0)
    z_to_x(1)
    w1_to_z(1)
    for u in range(2):
        for q in range(PLANES):
            frame_copy(u, q).wait()
    for j in range(1, LAYERS):
        g_copy(j).wait_recv()

    own_saved = LAYERS - 1 - sec
    pair_saved = LAYERS - 1 - pair[0]

    def out_at(ref, m, q):
        return ref.at[0, m, 0, :, pl.ds(q * QD, QD)]

    def own_save(l, u, q):
        return pltpu.make_async_copy(xs.at[l, u, q], out_at(out, 2 * zl + u, q), ol.at[u, q])

    def pair_save(l, u, q):
        return remote(xs.at[l, u, q], out_at(out, 2 * zl + u, q), os_.at[u, q], or_.at[u, q], pair)

    top = xs.at[LAYERS]

    def last_copy(u):
        return remote(
            top.at[u, y],
            out.at[0, 2 * zl + u, 0, :, pl.ds(pl.multiple_of(y * QD, QD), QD)],
            ls.at[u], lr.at[u, zl, y], (0, dp),
        )

    def far_half(u, i):
        half = top.at[u, 2, i * HF:(i + 1) * HF]
        return remote(half, half, hs.at[u, i], hr.at[u], (2 + 4 * i, dp))

    def far_whole(u):
        return remote(top.at[u, 2], top.at[u, 3], ls.at[u], fr.at[u], (2, dp))

    def near_whole(u):
        return remote(top.at[u, 1], top.at[u, 1], ls.at[u], fr.at[u], (1, dp))

    def half_on(u):
        i = y // 2
        part = pl.ds(pl.multiple_of(i * HF, HF), HF)
        return remote(
            top.at[u, 2, part], out.at[0, u, 0, part, 2 * QD:3 * QD], hs.at[u, 0], rr.at[u, i], (0, dp)
        )

    def far_on(u):
        return remote(top.at[u, 3], out_at(out, 2 + u, 2), hs.at[u, 1], lr.at[u, 1, 2], (0, dp))

    def near_on(u):
        return remote(top.at[u, 1], out_at(out, 2 + u, 1), hs.at[u, 1], lr.at[u, 1, 1], (0, dp))

    def half_arrival(u, i):
        return remote(
            top.at[u, 2, i * HF:(i + 1) * HF], out.at[0, u, 0, i * HF:(i + 1) * HF, 2 * QD:3 * QD],
            hs.at[u, 0], rr.at[u, i], (1, dp),
        )

    direct = (sec == 1) | (sec == 2) | (sec > 5)
    halves_on = (sec == 2) | (sec == 6)

    def last_own(u):
        return pltpu.make_async_copy(xs.at[LAYERS, u, 0], out_at(out, u, 0), ls.at[u])

    def last_arrival(u, zz, q):
        return remote(
            xs.at[LAYERS, u, q], out_at(out, 2 * zz + u, q), ls.at[u], lr.at[u, zz, q], (1, dp)
        )

    def saves(l, first, last):
        def due(saved):
            return (saved >= first) & (saved <= last) & (l == 6)

        for u in range(2):
            @pl.when(due(own_saved) | (own_saved == 6) & (first == 5) & (l == 7))
            def _():
                for q in range(PLANES):
                    own_save(own_saved + 1, u, q).start()

            @pl.when(due(pair_saved))
            def _():
                for q in range(PLANES):
                    pair_save(pair_saved + 1, u, q).start()

    def late_copy(u):
        return remote(
            xs.at[LAYERS - 1, u, y],
            out.at[0, 2 * zl + u, 0, :, pl.ds(pl.multiple_of(y * QD, QD), QD)],
            es.at[u], er.at[u, y], (1, dp),
        )

    def late_far(u):
        return remote(xs.at[LAYERS - 1, u, 2], xs.at[LAYERS, u, 0], es.at[u], fr.at[u], (7, dp))

    def late_on(u):
        return remote(xs.at[LAYERS, u, 0], out_at(out, u, 2), hs.at[u, 1], er.at[u, 2], (1, dp))

    def late_arrival(u, q):
        return remote(
            xs.at[LAYERS - 1, u, q], out_at(out, u, q), es.at[u], er.at[u, q], (0, dp)
        )

    rows = lax.broadcasted_iota(jnp.int32, (FR, FR), 0)
    cols = lax.broadcasted_iota(jnp.int32, (FR, FR), 1)
    keep = (cols < rows) | ((rows == 0) & (cols == 0))

    def compute(l, u):
        parts = [xs[l, u, q].astype(F32) for q in range(PLANES)]
        square = sum(jnp.sum(p * p, axis=-1, keepdims=True) for p in parts)
        scale = lax.rsqrt(square * (1.0 / D) + 1e-05)
        for q in range(PLANES):
            nrm[q] = (parts[q] * scale * gt[l, 0:1, q * QD:(q + 1) * QD]).astype(BF16)
        lhs = jnp.concatenate([nrm[q] for q in range(PLANES)], axis=1)
        proj = jnp.dot(lhs, w[l].reshape(D, QD), preferred_element_type=F32).astype(BF16)
        values = nrm[y]
        temper = gt[l, 1:2, pl.ds(pl.multiple_of(y * QD, QD), QD)]
        heads = [proj[:, k * HEAD:(k + 1) * HEAD] for k in range(QH)]
        scores = [
            lax.dot_general(h, h, (((1,), (1,)), ((), ())), preferred_element_type=F32) for h in heads
        ]
        scores = [
            jnp.where(keep, s * temper[:, k * HEAD:(k + 1) * HEAD], -1e30) for k, s in enumerate(scores)
        ]
        tops = [jnp.max(s, axis=-1, keepdims=True) for s in scores]
        expo = [jnp.exp(s - t) for s, t in zip(scores, tops)]
        sums = [jnp.sum(e, axis=-1, keepdims=True) for e in expo]
        weights = [(e / s).astype(BF16) for e, s in zip(expo, sums)]
        mixed = [
            jnp.dot(wt, values[:, k * HEAD:(k + 1) * HEAD], preferred_element_type=F32)
            for k, wt in enumerate(weights)
        ]
        xs[l + 1, u, y] = (xs[l, u, y].astype(F32) + jnp.concatenate(mixed, axis=1)).astype(BF16)

    def state_in(l, u):
        @pl.when(l > 0)
        def _():
            for i in range(2):
                y1_copy(l, u, i).wait_recv()
                y2_copy(l, u, i).start()

    def step(l, u):
        @pl.when(l > 0)
        def _():
            for i in range(2):
                y2_copy(l, u, i).wait_recv()

        compute(l, u)

        @pl.when((l == LAYERS - 1) & (sec == 0))
        def _():
            last_own(u).start()

        @pl.when((l == LAYERS - 1) & direct)
        def _():
            last_copy(u).start()

        @pl.when((l == LAYERS - 1) & (sec == 4))
        def _():
            for i in range(2):
                far_half(u, i).start()

        @pl.when((l == LAYERS - 1) & (sec == 5))
        def _():
            far_whole(u).start()

        @pl.when((l == LAYERS - 1) & (sec == 3))
        def _():
            near_whole(u).start()

        @pl.when(l + 1 < LAYERS)
        def _():
            for i in range(2):
                y1_copy(l + 1, u, i).start()

    def ahead(l):
        @pl.when(l + 2 < LAYERS)
        def _():
            z_to_x(l + 2)

        for p in (2, 3):
            @pl.when(l + 2 == 2 * p - 2)
            def _():
                w1_to_z(p)

    def layer(l, carry):
        x2_to_c(l)
        saves(l, 0, 4)
        state_in(l, 0)

        @pl.when((l > 0) & (l + 1 < LAYERS))
        def _():
            x1_to_x2(l + 1)

        state_in(l, 1)
        for d in range(NX):
            c_copy(l, d).wait_recv()
        step(l, 0)

        @pl.when(l == 0)
        def _():
            x1_to_x2(1)

        ahead(l)

        @pl.when((l == LAYERS - 1) & (zl == 0) & (y != 2))
        def _():
            for v in range(2):
                late_copy(v).start()

        @pl.when((l == LAYERS - 1) & (sec == 4))
        def _():
            for v in range(2):
                late_far(v).start()

        step(l, 1)
        saves(l, 5, 5)
        return carry

    lax.fori_loop(0, LAYERS, layer, 0)

    for u in range(2):
        @pl.when(sec == 7)
        def _():
            late_far(u).wait_recv()
            late_on(u).start()

        @pl.when(halves_on)
        def _():
            far_half(u, 0).wait_recv()
            half_on(u).start()

        @pl.when(sec == 2)
        def _():
            far_whole(u).wait_recv()
            far_on(u).start()

        @pl.when(sec == 1)
        def _():
            near_whole(u).wait_recv()
            near_on(u).start()

    for d in range(1, PLANES):
        w1_copy(d).wait_send()
    for j in range(1, LAYERS):
        g_copy(j).wait_send()
    for p in range(4):
        z_sends(p, lambda copy: copy.wait_send())

    def drain(l, carry):
        @pl.when((l % 2 == 1) | works)
        def _():
            for i in range(2):
                x1_copy(l, i).wait_send()
                x2_copy(l, i).wait_send()

        @pl.when((l % 2 == 0) & works)
        def _():
            for i in range(2):
                for d in range(NX):
                    p_copy(l, i, d).wait_send()

        for d in range(NX):
            c_copy(l, d).wait_send()

        @pl.when(l > 0)
        def _():
            for u in range(2):
                for i in range(2):
                    y1_copy(l, u, i).wait_send()
                    y2_copy(l, u, i).wait_send()

        return carry

    lax.fori_loop(0, LAYERS, drain, 0)

    @pl.when(sec != 0)
    def _():
        for u in range(2):
            for q in range(PLANES):
                own_save(0, u, q).wait()

    @pl.when(direct)
    def _():
        for u in range(2):
            last_copy(u).wait_send()

    @pl.when(sec == 4)
    def _():
        for u in range(2):
            for i in range(2):
                far_half(u, i).wait_send()

    @pl.when(sec == 5)
    def _():
        for u in range(2):
            far_whole(u).wait_send()

    @pl.when(sec == 3)
    def _():
        for u in range(2):
            near_whole(u).wait_send()

    @pl.when(sec == 2)
    def _():
        for u in range(2):
            far_on(u).wait_send()

    @pl.when(halves_on)
    def _():
        for u in range(2):
            half_on(u).wait_send()

    @pl.when(sec == 1)
    def _():
        for u in range(2):
            near_on(u).wait_send()

    @pl.when(sec > 1)
    def _():
        for u in range(2):
            for q in range(PLANES):
                pair_save(0, u, q).wait_send()
                pair_save(0, u, q).wait_recv()

    @pl.when((zl == 0) & (y != 2))
    def _():
        for u in range(2):
            late_copy(u).wait_send()

    @pl.when(sec == 4)
    def _():
        for u in range(2):
            late_far(u).wait_send()

    @pl.when(sec == 7)
    def _():
        for u in range(2):
            late_on(u).wait_send()

    @pl.when(sec == 1)
    def _():
        for u in range(2):
            for q in range(PLANES):
                late_arrival(u, q).wait_recv()

    @pl.when(sec == 0)
    def _():
        for u in range(2):
            last_own(u).wait()
            for zz in range(2):
                for q in range(PLANES):
                    if (zz, q) not in ((0, 0), (0, 2)):
                        last_arrival(u, zz, q).wait_recv()
            for i in range(2):
                half_arrival(u, i).wait_recv()


def local(frames, gains, w_shared, temper):
    dma = pltpu.SemaphoreType.DMA
    any_space = pl.BlockSpec(memory_space=pl.ANY)
    return pl.pallas_call(
        kernel,
        out_shape=jax.ShapeDtypeStruct((1,) + frames.shape, BF16),
        in_specs=[any_space, any_space] + [pl.BlockSpec(memory_space=pltpu.VMEM)] * 2,
        out_specs=any_space,
        scratch_shapes=[
            pltpu.VMEM((LAYERS, NZH, NX, 2, ROWS, QD), BF16),
            pltpu.VMEM((PLANES, ROWS, QD), BF16),
            pltpu.VMEM((LAYERS + 1, 2, PLANES, FR, QD), BF16),
            pltpu.VMEM((PLANES, FR, QD), BF16),
            pltpu.VMEM((LAYERS, 2, D), F32),
            dma((4,)), dma((3,)), dma((4,)),
            dma((4, 7)), dma((LAYERS, NZH)),
            dma((LAYERS, 2)), dma((LAYERS, 2)),
            dma((LAYERS, 2)), dma((LAYERS, 2)),
            dma((LAYERS // 2, 2, NX)), dma((LAYERS // 2, 2, NX)),
            dma((LAYERS, 4)), dma((LAYERS, 4)),
            dma((LAYERS, 2, 2)), dma((LAYERS, 2, 2)),
            dma((LAYERS, 2, 2)), dma((LAYERS, 2, 2)),
            dma((LAYERS - 1,)), dma((LAYERS - 1,)),
            dma((2, PLANES)), dma((2, PLANES)),
            dma((2, PLANES)), dma((2, PLANES)),
            dma((2,)), dma((2, 2, PLANES)),
            dma((2,)), dma((2, PLANES)),
            dma((2, 2)), dma((2,)), dma((2, 2)), dma((2,)),
        ],
        compiler_params=pltpu.CompilerParams(
            collective_id=0, has_side_effects=True, vmem_limit_bytes=58 << 20
        ),
    )(frames, w_shared, gains, temper)


def solution(mesh):
    in_specs = (
        P(None, "dp", None, None),
        P("section", None),
        P("section", "dp", None),
        P("section", None),
    )
    out_specs = P("section", None, "dp", None, None)
    return jax.shard_map(local, mesh=mesh, in_specs=in_specs, out_specs=out_specs, check_vma=False)
```
